128 devices in a mesh: ops: 8 (over x, core), sec: 16 (over y, z).
Axes of the slice: x: 4, y: 4, z: 4, core: 2. Of those that a mesh axis runs over, the one named last changes fastest.
Arguments:
- psi: bfloat16 [16, 16, 512, 512], P(None, 'sec'), may hold values from -6 to 6
- left_ops: bfloat16 [8, 16, 512, 512], P('ops'), may hold values from -0.25 to 0.25
- left_src: int32 [8, 16], P('ops'), may hold values from 0 to 15
- right_ops: bfloat16 [8, 16, 512, 512], P('ops'), may hold values from -0.125 to 0.125
- right_src: int32 [8, 16], P('ops'), may hold values from 0 to 15
- left_parity: int32 [16], replicated, may hold values from 0 to 1
- right_parity: int32 [16], replicated, may hold values from 0 to 1
Outputs:
- sigma: bfloat16 [16, 16, 512, 512], P('sec', 'ops')
The draws below stay inside these ranges and needn't reach their ends.
All inputs are finite; a program needn't handle non-finite values.
Results may differ from the reference program's by a relative error of at most 0.015.
Values may be sent and summed in bfloat16 or wider, within the bound.
No kernel may reach another device: no remote copies, remote signals or barrier semaphores. Data moves between devices by JAX's collectives and lax.ppermute only.
A program may use at most 128 MiB of HBM per device.

```python
import jax
import jax.numpy as jnp
from jax import lax

M = 512
G_DEV = 1
K = 16
G = 8
N_OPS = 8


def place_ends(result, own_key, low, high):
    longest = result.shape.index(max(result.shape))
    spots = []
    for shift in (0, 1):
        where = [jax.random.randint(jax.random.fold_in(own_key, axis), (), 0, length) for axis, length in enumerate(result.shape)]
        where[longest] = (where[longest] + shift) % result.shape[longest]
        spots.append(tuple(where))
    return result.at[spots[0]].set(low).at[spots[1]].set(high)


def raised(result, own_key, source, target, shards_of, factor):
    owner, partner = [(jnp.arange(result.shape[axis_at]) // (result.shape[axis_at] // shards_of)).reshape([-1 if axis == axis_at else 1 for axis in range(result.ndim)]) for axis_at in (source, target)]
    chosen = jax.random.permutation(own_key, shards_of)[partner]
    strong = (owner == chosen) | (owner == (partner + shards_of // 2) % shards_of)
    return jnp.where(strong, factor * result, result)


def level_of(own_key, dims, cuts, smallest, top_value):
    gain = 1.0
    for axis_at, shards_of in cuts:
        heights = jax.random.uniform(jax.random.fold_in(jax.random.fold_in(own_key, 6), axis_at), (shards_of,), jnp.float32, smallest / len(cuts), top_value / len(cuts))
        gain = gain * jnp.repeat(jnp.exp(heights), dims[axis_at] // shards_of).reshape((-1,) + (1,) * (len(dims) - 1 - axis_at))
    return gain


def centred(key, extent, width, most, split=(), held_as=jnp.bfloat16):
    loudness = level_of(key, extent, split, -0.22, 0.18) if split else 1.0
    entries = jax.random.normal(key, extent, jnp.float32) * width * loudness
    return jnp.minimum(jnp.maximum(entries, -most), most).astype(held_as)


def heavy_noise(key, extent, width, limit, shards, heavy, kind=jnp.bfloat16):
    entries = width * jax.random.normal(key, extent, jnp.float32)
    if shards:
        entries = entries * level_of(key, extent, shards, -0.22, 0.18)
    return jnp.clip(raised(entries, jax.random.fold_in(key, 3), *heavy), -limit, limit).astype(kind)


def setup_inputs(seed: int = 0) -> dict:
    seeds = jax.random.split(jax.random.key(seed), 8)
    return {
        "psi": centred(seeds[0], (K, K, M, M), 1.0, 6.0, ((1, 16),)),
        "left_ops": centred(seeds[1], (G, K, M, M), M ** -0.5, 0.25, ((0, 8),)),
        "left_src": place_ends(jax.random.randint(seeds[2], (G, K), 0, K), jax.random.fold_in(seeds[2], 1), 0, K - 1).astype(jnp.int32),
        "right_ops": heavy_noise(seeds[3], (G, K, M, M), (M * G) ** -0.5, 0.125, ((0, 8),), (0, 1, 8, 2.0)),
        "right_src": place_ends(jax.random.randint(seeds[4], (G, K), 0, K), jax.random.fold_in(seeds[4], 1), 0, K - 1).astype(jnp.int32),
        "left_parity": place_ends(jax.random.randint(seeds[5], (K,), 0, 2), jax.random.fold_in(seeds[5], 1), 0, 1).astype(jnp.int32),
        "right_parity": place_ends(jax.random.randint(seeds[6], (K,), 0, 2), jax.random.fold_in(seeds[6], 1), 0, 1).astype(jnp.int32),
    }


def group_term(masked, left_block, left_rows, right_block, right_cols):
    rows = jnp.take(masked, left_rows, axis=0).astype(jnp.float32)
    contracted = jnp.einsum("iab,ikbc->ikac", left_block.astype(jnp.float32), rows).astype(jnp.bfloat16)
    picked = jnp.take(contracted, right_cols, axis=1).astype(jnp.float32)
    return jnp.einsum("ikab,kcb->ikac", picked, right_block.astype(jnp.float32))


def reference(psi, left_ops, left_src, right_ops, right_src, left_parity, right_parity):
    live = (left_parity[:, None] + right_parity[None, :]) % 2 == 1
    masked = jnp.where(live[:, :, None, None], psi, jnp.zeros_like(psi))

    def device_step(total, device):
        partial_value = jnp.zeros(psi.shape, jnp.float32)
        for member in range(G_DEV):
            group = (device * G_DEV + member).astype(jnp.int32)
            partial_value = partial_value + group_term(masked, left_ops[group], left_src[group], right_ops[group], right_src[group])
        rounded = lax.optimization_barrier(partial_value.astype(jnp.bfloat16))
        return total + rounded.astype(jnp.float32), None

    start_total = jnp.zeros(psi.shape, jnp.float32)
    total, unused = lax.scan(device_step, start_total, jnp.arange(N_OPS, dtype=jnp.int32))
    sigma = jnp.where(live[:, :, None, None], total, jnp.zeros_like(total))
    return sigma.astype(jnp.bfloat16)
```

```python
import jax
import jax.numpy as jnp
from jax import lax
from jax.experimental import pallas as pl
from jax.experimental.pallas import tpu as pltpu
from jax.sharding import PartitionSpec as P

CHUNKS = (320, 192)
F32 = jnp.float32
BF16 = jnp.bfloat16
MIB = 1024 * 1024


def left_kernel(me, ls, rs, lp, rp, psi, left, *rest):
    outs = rest[: len(CHUNKS)]
    items, pbuf, lbuf, obuf, psem, lsem, osem = rest[len(CHUNKS):]
    sectors = psi.shape[0]
    col = me[0]
    col_parity = rp[col] & 1

    def scan(k, flags):
        hit = (rs[k] == col).astype(jnp.int32)
        odd = rp[k] & 1
        return flags[0] | (hit * odd), flags[1] | (hit * (1 - odd))

    for_even, for_odd = lax.fori_loop(0, sectors, scan, (jnp.int32(0), jnp.int32(0)))

    def fetch(i, count):
        source = ls[i]
        wanted = jnp.where((lp[i] & 1) == 1, for_odd, for_even)
        need = (wanted == 1) & ((lp[source] & 1) != col_parity)

        @pl.when(need)
        def _():
            items[count] = i
            pltpu.make_async_copy(psi.at[source], pbuf.at[count], psem.at[count]).start()
            pltpu.make_async_copy(left.at[i], lbuf.at[count], lsem.at[count]).start()

        return count + need.astype(jnp.int32)

    count = lax.fori_loop(0, sectors, fetch, jnp.int32(0))

    def stores(j):
        at = 0
        for c, rows in enumerate(CHUNKS):
            yield pltpu.make_async_copy(
                obuf.at[j, pl.ds(at, rows)], outs[c].at[items[j]], osem.at[c, j]
            )
            at += rows

    def work(j, carry):
        pltpu.make_async_copy(psi.at[0], pbuf.at[j], psem.at[j]).wait()
        pltpu.make_async_copy(left.at[0], lbuf.at[j], lsem.at[j]).wait()
        obuf[j] = jnp.dot(lbuf[j], pbuf[j], preferred_element_type=F32).astype(BF16)
        for copy in stores(j):
            copy.start()
        return carry

    lax.fori_loop(0, count, work, 0)

    def finish(j, carry):
        for copy in stores(j):
            copy.wait()
        return carry

    lax.fori_loop(0, count, finish, 0)


def left_products(me, ls, rs, lp, rp, psi, left):
    k, m = psi.shape[0], psi.shape[-1]
    smem = pl.BlockSpec(memory_space=pltpu.SMEM)
    hbm = pl.BlockSpec(memory_space=pl.ANY)
    return pl.pallas_call(
        left_kernel,
        out_shape=[jax.ShapeDtypeStruct((k, rows, m), BF16) for rows in CHUNKS],
        in_specs=[smem] * 5 + [hbm] * 2,
        out_specs=[hbm] * len(CHUNKS),
        scratch_shapes=[
            pltpu.SMEM((k,), jnp.int32),
            pltpu.VMEM((k, m, m), BF16),
            pltpu.VMEM((k, m, m), BF16),
            pltpu.VMEM((k, m, m), BF16),
            pltpu.SemaphoreType.DMA((k,)),
            pltpu.SemaphoreType.DMA((k,)),
            pltpu.SemaphoreType.DMA((len(CHUNKS), k)),
        ],
        compiler_params=pltpu.CompilerParams(vmem_limit_bytes=40 * MIB),
        cost_estimate=pl.CostEstimate(
            flops=8 * m ** 3, bytes_accessed=12 * m * m * 2, transcendentals=0
        ),
        name="left_products",
    )(me, ls, rs, lp, rp, psi, left)


def right_kernel(me, ls, rs, lp, rp, block, right, keep, give, items, zbuf, sbuf, rbuf, obuf, ssem, rsem, osem, zsem):
    sectors = right.shape[0]
    row, core = me[0], me[1]
    row_parity = lp[row] & 1
    source_parity = lp[ls[row]] & 1

    def fetch(k, count):
        live = (rp[k] & 1) != row_parity
        source = rs[k]
        need = live & ((rp[source] & 1) != source_parity)

        @pl.when(need)
        def _():
            items[count] = k
            pltpu.make_async_copy(block.at[source], sbuf.at[count], ssem.at[count]).start()
            pltpu.make_async_copy(right.at[k], rbuf.at[count], rsem.at[count]).start()

        return count + need.astype(jnp.int32)

    count = lax.fori_loop(0, sectors, fetch, jnp.int32(0))

    def place(buf, k, sem, act):
        slot = (k // 4) * 2 + k % 2
        mine = (k // 2) % 2 == core

        @pl.when(mine)
        def _():
            act(pltpu.make_async_copy(buf, keep.at[slot], sem))

        @pl.when(jnp.logical_not(mine))
        def _():
            act(pltpu.make_async_copy(buf, give.at[slot], sem))

    zbuf[...] = jnp.zeros_like(zbuf)

    def empty(k):
        return ((rp[k] & 1) != row_parity) & ((rp[rs[k]] & 1) == source_parity)

    def clear(k, carry):
        @pl.when(empty(k))
        def _():
            place(zbuf, k, zsem.at[k], lambda copy: copy.start())

        return carry

    lax.fori_loop(0, sectors, clear, 0)

    def work(j, carry):
        pltpu.make_async_copy(block.at[0], sbuf.at[j], ssem.at[j]).wait()
        pltpu.make_async_copy(right.at[0], rbuf.at[j], rsem.at[j]).wait()
        obuf[j] = lax.dot_general(
            sbuf[j], rbuf[j], (((1,), (1,)), ((), ())), preferred_element_type=F32
        ).astype(BF16)
        place(obuf.at[j], items[j], osem.at[j], lambda copy: copy.start())
        return carry

    lax.fori_loop(0, count, work, 0)

    def finish(j, carry):
        place(obuf.at[j], items[j], osem.at[j], lambda copy: copy.wait())
        return carry

    lax.fori_loop(0, count, finish, 0)

    def cleared(k, carry):
        @pl.when(empty(k))
        def _():
            place(zbuf, k, zsem.at[k], lambda copy: copy.wait())

        return carry

    lax.fori_loop(0, sectors, cleared, 0)


def right_products(me, ls, rs, lp, rp, block, right):
    k, rows, m = block.shape
    smem = pl.BlockSpec(memory_space=pltpu.SMEM)
    hbm = pl.BlockSpec(memory_space=pl.ANY)
    half = jax.ShapeDtypeStruct((k // 2, rows, m), BF16)
    return pl.pallas_call(
        right_kernel,
        out_shape=[half, half],
        in_specs=[smem] * 5 + [hbm] * 2,
        out_specs=[hbm] * 2,
        scratch_shapes=[
            pltpu.SMEM((k,), jnp.int32),
            pltpu.VMEM((rows, m), BF16),
            pltpu.VMEM((k, rows, m), BF16),
            pltpu.VMEM((k, m, m), BF16),
            pltpu.VMEM((k, rows, m), BF16),
            pltpu.SemaphoreType.DMA((k,)),
            pltpu.SemaphoreType.DMA((k,)),
            pltpu.SemaphoreType.DMA((k,)),
            pltpu.SemaphoreType.DMA((k,)),
        ],
        compiler_params=pltpu.CompilerParams(vmem_limit_bytes=40 * MIB),
        cost_estimate=pl.CostEstimate(
            flops=16 * rows * m * m, bytes_accessed=8 * m * m * 2 + 16 * rows * m * 2, transcendentals=0
        ),
        name="right_products",
    )(me, ls, rs, lp, rp, block, right)


def summed_over_ops(keep, give):
    n = 8
    got = lax.ppermute(give, "ops", [(o, o ^ 1) for o in range(n)])
    pair = (keep.astype(F32) + got.astype(F32)).astype(BF16)
    chip = lax.axis_index("ops") // 2
    total = lax.dynamic_slice_in_dim(pair, chip * 2, 2).astype(F32)
    for hop in (1, 2, 3):
        part = lax.dynamic_slice_in_dim(pair, (chip + hop) % 4 * 2, 2)
        part = lax.ppermute(part, "ops", [(o, (o + 2 * hop) % n) for o in range(n)])
        total = total + part.astype(F32)
    return total


def local(psi, left_ops, left_src, right_ops, right_src, left_parity, right_parity):
    sec, ops = lax.axis_index("sec"), lax.axis_index("ops")
    me = jnp.stack([sec, ops % 2]).astype(jnp.int32)
    ls, rs = left_src[0], right_src[0]
    sends = left_products(me, ls, rs, left_parity, right_parity, psi[:, 0], left_ops[0])
    sums = []
    for send in sends:
        block = lax.all_to_all(send, "sec", 0, 0, tiled=True)
        keep, give = right_products(me, ls, rs, left_parity, right_parity, block, right_ops[0])
        sums.append(summed_over_ops(keep, give))
    row_parity = lax.dynamic_slice_in_dim(left_parity, sec, 1)
    out_parity = lax.dynamic_slice_in_dim(right_parity, ops * 2, 2)
    live = ((out_parity + row_parity) % 2 == 1)[:, None, None]
    result = jnp.concatenate([jnp.where(live, s, 0.0).astype(BF16) for s in sums], axis=1)
    return result[None]


def solution(mesh):
    placed = (
        P(None, "sec", None, None),
        P("ops", None, None, None),
        P("ops", None),
        P("ops", None, None, None),
        P("ops", None),
        P(),
        P(),
    )
    return jax.shard_map(
        local, mesh=mesh, in_specs=placed, out_specs=P("sec", "ops", None, None), check_vma=False
    )
```

```python
import functools

import jax
import jax.numpy as jnp
from jax import lax
from jax.experimental import pallas as pl
from jax.experimental.pallas import tpu as pltpu
from jax.sharding import PartitionSpec as P

CHUNKS = (320, 192)
F32 = jnp.float32
BF16 = jnp.bfloat16
MIB = 1024 * 1024
HBM = pl.BlockSpec(memory_space=pl.ANY)


def read_lists(given, held, sem):
    copies = [pltpu.make_async_copy(g, h, sem.at[n]) for n, (g, h) in enumerate(zip(given, held))]
    for copy in copies:
        copy.start()
    for copy in copies:
        copy.wait()


def list_scratch(k):
    return [pltpu.SMEM((k,), jnp.int32)] * 4 + [pltpu.SemaphoreType.DMA((4,))]


def left_kernel(*refs):
    lists, (psi, left), outs = refs[:4], refs[4:6], refs[6 : 6 + len(CHUNKS)]
    held, list_sem, items, pbuf, lbuf, obuf, psem, lsem, osem = refs[6 + len(CHUNKS):][:4], *refs[10 + len(CHUNKS):]
    read_lists(lists, held, list_sem)
    ls, rs, lp, rp = held
    sectors = psi.shape[0]
    col = lax.axis_index("sec")
    col_parity = rp[col] & 1

    def scan(k, flags):
        hit = (rs[k] == col).astype(jnp.int32)
        odd = rp[k] & 1
        return flags[0] | (hit * odd), flags[1] | (hit * (1 - odd))

    for_even, for_odd = lax.fori_loop(0, sectors, scan, (jnp.int32(0), jnp.int32(0)))

    def fetch(i, count):
        source = ls[i]
        wanted = jnp.where((lp[i] & 1) == 1, for_odd, for_even)
        need = (wanted == 1) & ((lp[source] & 1) != col_parity)

        @pl.when(need)
        def _():
            items[count] = i
            pltpu.make_async_copy(psi.at[source], pbuf.at[count], psem.at[count]).start()
            pltpu.make_async_copy(left.at[i], lbuf.at[count], lsem.at[count]).start()

        return count + need.astype(jnp.int32)

    count = lax.fori_loop(0, sectors, fetch, jnp.int32(0))

    def stores(j):
        at = 0
        for c, rows in enumerate(CHUNKS):
            yield pltpu.make_async_copy(
                obuf.at[j, pl.ds(at, rows)], outs[c].at[items[j]], osem.at[c, j]
            )
            at += rows

    def work(j, carry):
        pltpu.make_async_copy(psi.at[0], pbuf.at[j], psem.at[j]).wait()
        pltpu.make_async_copy(left.at[0], lbuf.at[j], lsem.at[j]).wait()
        obuf[j] = jnp.dot(lbuf[j], pbuf[j], preferred_element_type=F32).astype(BF16)
        for copy in stores(j):
            copy.start()
        return carry

    lax.fori_loop(0, count, work, 0)

    def finish(j, carry):
        for copy in stores(j):
            copy.wait()
        return carry

    lax.fori_loop(0, count, finish, 0)


def left_products(lists, psi, left):
    k, m = psi.shape[0], psi.shape[-1]
    return pl.pallas_call(
        left_kernel,
        out_shape=[jax.ShapeDtypeStruct((k, rows, m), BF16) for rows in CHUNKS],
        in_specs=[HBM] * 6,
        out_specs=[HBM] * len(CHUNKS),
        scratch_shapes=list_scratch(k) + [
            pltpu.SMEM((k,), jnp.int32),
            pltpu.VMEM((k, m, m), BF16),
            pltpu.VMEM((k, m, m), BF16),
            pltpu.VMEM((k, m, m), BF16),
            pltpu.SemaphoreType.DMA((k,)),
            pltpu.SemaphoreType.DMA((k,)),
            pltpu.SemaphoreType.DMA((len(CHUNKS), k)),
        ],
        compiler_params=pltpu.CompilerParams(vmem_limit_bytes=56 * MIB),
        cost_estimate=pl.CostEstimate(
            flops=8 * m ** 3, bytes_accessed=12 * m * m * 2, transcendentals=0
        ),
        name="left_products",
    )(*lists, psi, left)


def right_kernel(first, *refs):
    lists, (block, right, keep, give), refs = refs[:4], refs[4:8], refs[8:]
    if first:
        turned, refs = refs[0], refs[1:]
    held, (list_sem, items, zbuf, sbuf, rbuf, obuf, ssem, rsem, osem), refs = refs[:4], refs[4:13], refs[13:]
    if first:
        tbuf, tsem = refs
    read_lists(lists, held, list_sem)
    ls, rs, lp, rp = held
    sectors = right.shape[0]
    row, core = lax.axis_index("sec"), lax.axis_index("ops") % 2
    row_parity = lp[row] & 1
    source_parity = lp[ls[row]] & 1
    zbuf[...] = jnp.zeros_like(zbuf)

    def place(buf, k):
        slot = (k // 4) * 2 + k % 2
        mine = (k // 2) % 2 == core

        @pl.when(mine)
        def _():
            pltpu.make_async_copy(buf, keep.at[slot], osem.at[k]).start()

        @pl.when(jnp.logical_not(mine))
        def _():
            pltpu.make_async_copy(buf, give.at[slot], osem.at[k]).start()

    def fetch(k, count):
        live = (rp[k] & 1) != row_parity
        source = rs[k]
        need = live & ((rp[source] & 1) != source_parity)

        @pl.when(need)
        def _():
            items[count] = k
            pltpu.make_async_copy(block.at[source], sbuf.at[count], ssem.at[count]).start()
            pltpu.make_async_copy(right.at[k], rbuf.at[count], rsem.at[count]).start()

        @pl.when(live & jnp.logical_not(need))
        def _():
            place(zbuf, k)

        return count + need.astype(jnp.int32)

    count = lax.fori_loop(0, sectors, fetch, jnp.int32(0))

    def work(j, carry):
        pltpu.make_async_copy(right.at[0], rbuf.at[j], rsem.at[j]).wait()
        if first:
            tbuf[j] = rbuf[j].T
            pltpu.make_async_copy(tbuf.at[j], turned.at[items[j]], tsem.at[j]).start()
        pltpu.make_async_copy(block.at[0], sbuf.at[j], ssem.at[j]).wait()
        factor = tbuf[j] if first else rbuf[j]
        obuf[j] = jnp.dot(sbuf[j], factor, preferred_element_type=F32).astype(BF16)
        place(obuf.at[j], items[j])
        return carry

    lax.fori_loop(0, count, work, 0)

    def finish(k, carry):
        @pl.when((rp[k] & 1) != row_parity)
        def _():
            pltpu.make_async_copy(zbuf, keep.at[0], osem.at[k]).wait()

        return carry

    lax.fori_loop(0, sectors, finish, 0)
    if first:
        def turn(j, carry):
            pltpu.make_async_copy(tbuf.at[j], turned.at[0], tsem.at[j]).wait()
            return carry

        lax.fori_loop(0, count, turn, 0)


def right_products(lists, block, right, first):
    k, rows, m = block.shape
    out = [jax.ShapeDtypeStruct((k // 2, rows, m), BF16)] * 2
    extra = []
    if first:
        out = out + [jax.ShapeDtypeStruct((k, m, m), BF16)]
        extra = [pltpu.VMEM((k, m, m), BF16), pltpu.SemaphoreType.DMA((k,))]
    return pl.pallas_call(
        functools.partial(right_kernel, first),
        out_shape=out,
        in_specs=[HBM] * 6,
        out_specs=[HBM] * len(out),
        scratch_shapes=list_scratch(k) + [
            pltpu.SMEM((k,), jnp.int32),
            pltpu.VMEM((rows, m), BF16),
            pltpu.VMEM((k, rows, m), BF16),
            pltpu.VMEM((k, m, m), BF16),
            pltpu.VMEM((k, rows, m), BF16),
            pltpu.SemaphoreType.DMA((k,)),
            pltpu.SemaphoreType.DMA((k,)),
            pltpu.SemaphoreType.DMA((k,)),
        ] + extra,
        compiler_params=pltpu.CompilerParams(vmem_limit_bytes=56 * MIB),
        cost_estimate=pl.CostEstimate(
            flops=16 * rows * m * m, bytes_accessed=8 * m * m * 2 + 16 * rows * m * 2, transcendentals=0
        ),
        name="right_products",
    )(*lists, block, right)


def summed_over_ops(keep, give):
    n = 8
    got = lax.ppermute(give, "ops", [(o, o ^ 1) for o in range(n)])
    pair = (keep.astype(F32) + got.astype(F32)).astype(BF16)
    chip = lax.axis_index("ops") // 2
    total = lax.dynamic_slice_in_dim(pair, chip * 2, 2).astype(F32)
    for hop in (1, 2, 3):
        part = lax.dynamic_slice_in_dim(pair, (chip + hop) % 4 * 2, 2)
        part = lax.ppermute(part, "ops", [(o, (o + 2 * hop) % n) for o in range(n)])
        total = total + part.astype(F32)
    return total


def local(psi, left_ops, left_src, right_ops, right_src, left_parity, right_parity):
    sec, ops = lax.axis_index("sec"), lax.axis_index("ops")
    lists = (left_src[0], right_src[0], left_parity, right_parity)
    row_parity = lax.dynamic_slice_in_dim(left_parity, sec, 1)
    out_parity = lax.dynamic_slice_in_dim(right_parity, ops * 2, 2)
    live = ((out_parity + row_parity) % 2 == 1)[:, None, None]
    sends = left_products(lists, psi[:, 0], left_ops[0])
    blocks = [lax.all_to_all(send, "sec", 0, 0, tiled=True) for send in sends]
    keep, give, turned = right_products(lists, blocks[0], right_ops[0], True)
    early = jnp.where(live, summed_over_ops(keep, give), 0.0).astype(BF16)
    early, last = lax.optimization_barrier((early, blocks[1]))
    keep, give = right_products(lists, last, turned, False)
    late = jnp.where(live, summed_over_ops(keep, give), 0.0).astype(BF16)
    return jnp.concatenate([early, late], axis=1)[None]


def solution(mesh):
    placed = (
        P(None, "sec", None, None),
        P("ops", None, None, None),
        P("ops", None),
        P("ops", None, None, None),
        P("ops", None),
        P(),
        P(),
    )
    return jax.shard_map(
        local, mesh=mesh, in_specs=placed, out_specs=P("sec", "ops", None, None), check_vma=False
    )
```

```python
import functools

import jax
import jax.numpy as jnp
from jax import lax
from jax.experimental import pallas as pl
from jax.experimental.pallas import tpu as pltpu
from jax.sharding import PartitionSpec as P

CHUNKS = (400, 112)
F32 = jnp.float32
BF16 = jnp.bfloat16
MIB = 1024 * 1024
AHEAD = 4
HBM = pl.BlockSpec(memory_space=pl.ANY)


def read_lists(given, held, sem):
    copies = [pltpu.make_async_copy(g, h, sem.at[n]) for n, (g, h) in enumerate(zip(given, held))]
    for copy in copies:
        copy.start()
    for copy in copies:
        copy.wait()


def list_scratch(k):
    return [pltpu.SMEM((k,), jnp.int32)] * 4 + [pltpu.SemaphoreType.DMA((4,))]


def left_kernel(*refs):
    lists, (psi, left), outs = refs[:4], refs[4:6], refs[6 : 6 + len(CHUNKS)]
    held, list_sem, items, pbuf, lbuf, obuf, psem, lsem, osem = refs[6 + len(CHUNKS):][:4], *refs[10 + len(CHUNKS):]
    read_lists(lists, held, list_sem)
    ls, rs, lp, rp = held
    sectors = psi.shape[0]
    col = lax.axis_index("sec")
    col_parity = rp[col] & 1

    def scan(k, flags):
        hit = (rs[k] == col).astype(jnp.int32)
        odd = rp[k] & 1
        return flags[0] | (hit * odd), flags[1] | (hit * (1 - odd))

    for_even, for_odd = lax.fori_loop(0, sectors, scan, (jnp.int32(0), jnp.int32(0)))

    def pick(i, count):
        wanted = jnp.where((lp[i] & 1) == 1, for_odd, for_even)
        need = (wanted == 1) & ((lp[ls[i]] & 1) != col_parity)

        @pl.when(need)
        def _():
            items[count] = i

        return count + need.astype(jnp.int32)

    count = lax.fori_loop(0, sectors, pick, jnp.int32(0))

    def fetch(j, carry=0):
        i = items[j]
        pltpu.make_async_copy(psi.at[ls[i]], pbuf.at[j], psem.at[j]).start()
        pltpu.make_async_copy(left.at[i], lbuf.at[j], lsem.at[j]).start()
        return carry

    lax.fori_loop(0, jnp.minimum(count, AHEAD), fetch, 0)

    def stores(j):
        at = 0
        for c, rows in enumerate(CHUNKS):
            yield pltpu.make_async_copy(
                obuf.at[j, pl.ds(at, rows)], outs[c].at[items[j]], osem.at[c, j]
            )
            at += rows

    def work(j, carry):
        @pl.when(j + AHEAD < count)
        def _():
            fetch(j + AHEAD)

        pltpu.make_async_copy(psi.at[0], pbuf.at[j], psem.at[j]).wait()
        pltpu.make_async_copy(left.at[0], lbuf.at[j], lsem.at[j]).wait()
        obuf[j] = jnp.dot(lbuf[j], pbuf[j], preferred_element_type=F32).astype(BF16)
        for copy in stores(j):
            copy.start()
        return carry

    lax.fori_loop(0, count, work, 0)

    def finish(j, carry):
        for copy in stores(j):
            copy.wait()
        return carry

    lax.fori_loop(0, count, finish, 0)


def left_products(lists, psi, left):
    k, m = psi.shape[0], psi.shape[-1]
    return pl.pallas_call(
        left_kernel,
        out_shape=[jax.ShapeDtypeStruct((k, rows, m), BF16) for rows in CHUNKS],
        in_specs=[HBM] * 6,
        out_specs=[HBM] * len(CHUNKS),
        scratch_shapes=list_scratch(k) + [
            pltpu.SMEM((k,), jnp.int32),
            pltpu.VMEM((k, m, m), BF16),
            pltpu.VMEM((k, m, m), BF16),
            pltpu.VMEM((k, m, m), BF16),
            pltpu.SemaphoreType.DMA((k,)),
            pltpu.SemaphoreType.DMA((k,)),
            pltpu.SemaphoreType.DMA((len(CHUNKS), k)),
        ],
        compiler_params=pltpu.CompilerParams(vmem_limit_bytes=56 * MIB),
        cost_estimate=pl.CostEstimate(
            flops=8 * m ** 3, bytes_accessed=12 * m * m * 2, transcendentals=0
        ),
        name="left_products",
    )(*lists, psi, left)


def right_kernel(whole, *refs):
    n = 7 if whole else 8
    lists, (block, right), outs, refs = refs[:4], refs[4:6], refs[6:n], refs[n:]
    held, (list_sem, items, zbuf, sbuf, rbuf, obuf, ssem, rsem, osem) = refs[:4], refs[4:]
    read_lists(lists, held, list_sem)
    ls, rs, lp, rp = held
    sectors = right.shape[0]
    row, core = lax.axis_index("sec"), lax.axis_index("ops") % 2
    row_parity = lp[row] & 1
    source_parity = lp[ls[row]] & 1
    zbuf[...] = jnp.zeros_like(zbuf)

    def place(buf, k):
        if whole:
            pltpu.make_async_copy(buf, outs[0].at[k], osem.at[k]).start()
            return
        keep, give = outs
        slot = (k // 4) * 2 + k % 2
        mine = (k // 2) % 2 == core

        @pl.when(mine)
        def _():
            pltpu.make_async_copy(buf, keep.at[slot], osem.at[k]).start()

        @pl.when(jnp.logical_not(mine))
        def _():
            pltpu.make_async_copy(buf, give.at[slot], osem.at[k]).start()

    def pick(k, count):
        live = (rp[k] & 1) != row_parity
        need = live & ((rp[rs[k]] & 1) != source_parity)

        @pl.when(need)
        def _():
            items[count] = k

        @pl.when(live & jnp.logical_not(need))
        def _():
            place(zbuf, k)

        return count + need.astype(jnp.int32)

    count = lax.fori_loop(0, sectors, pick, jnp.int32(0))

    def fetch(j, carry=0):
        k = items[j]
        pltpu.make_async_copy(right.at[k], rbuf.at[j], rsem.at[j]).start()
        pltpu.make_async_copy(block.at[rs[k]], sbuf.at[j], ssem.at[j]).start()
        return carry

    lax.fori_loop(0, jnp.minimum(count, AHEAD), fetch, 0)

    def work(j, carry):
        @pl.when(j + AHEAD < count)
        def _():
            fetch(j + AHEAD)

        pltpu.make_async_copy(right.at[0], rbuf.at[j], rsem.at[j]).wait()
        pltpu.make_async_copy(block.at[0], sbuf.at[j], ssem.at[j]).wait()
        obuf[j] = lax.dot_general(
            sbuf[j], rbuf[j], (((1,), (1,)), ((), ())), preferred_element_type=F32
        ).astype(BF16)
        place(obuf.at[j], items[j])
        return carry

    lax.fori_loop(0, count, work, 0)

    def finish(k, carry):
        @pl.when((rp[k] & 1) != row_parity)
        def _():
            pltpu.make_async_copy(zbuf, outs[0].at[0], osem.at[k]).wait()

        return carry

    lax.fori_loop(0, sectors, finish, 0)


def right_products(lists, block, right, whole):
    k, rows, m = block.shape
    out = [jax.ShapeDtypeStruct((k // 2, rows, m), BF16)] * 2
    if whole:
        out = [jax.ShapeDtypeStruct((k, rows, m), BF16)]
    return pl.pallas_call(
        functools.partial(right_kernel, whole),
        out_shape=out,
        in_specs=[HBM] * 6,
        out_specs=[HBM] * len(out),
        scratch_shapes=list_scratch(k) + [
            pltpu.SMEM((k,), jnp.int32),
            pltpu.VMEM((rows, m), BF16),
            pltpu.VMEM((k, rows, m), BF16),
            pltpu.VMEM((k, m, m), BF16),
            pltpu.VMEM((k, rows, m), BF16),
            pltpu.SemaphoreType.DMA((k,)),
            pltpu.SemaphoreType.DMA((k,)),
            pltpu.SemaphoreType.DMA((k,)),
        ],
        compiler_params=pltpu.CompilerParams(vmem_limit_bytes=61 * MIB),
        cost_estimate=pl.CostEstimate(
            flops=16 * rows * m * m, bytes_accessed=8 * m * m * 2 + 16 * rows * m * 2, transcendentals=0
        ),
        name="right_products",
    )(*lists, block, right)


def summed_over_ops(keep, give):
    n = 8
    got = lax.ppermute(give, "ops", [(o, o ^ 1) for o in range(n)])
    pair = (keep.astype(F32) + got.astype(F32)).astype(BF16)
    chip = lax.axis_index("ops") // 2
    total = lax.dynamic_slice_in_dim(pair, chip * 2, 2).astype(F32)
    for hop in (2, 1, 3):
        part = lax.dynamic_slice_in_dim(pair, (chip + hop) % 4 * 2, 2)
        part = lax.ppermute(part, "ops", [(o, (o + 2 * hop) % n) for o in range(n)])
        total = total + part.astype(F32)
    return total


def local(psi, left_ops, left_src, right_ops, right_src, left_parity, right_parity):
    sec, ops = lax.axis_index("sec"), lax.axis_index("ops")
    lists = (left_src[0], right_src[0], left_parity, right_parity)
    row_parity = lax.dynamic_slice_in_dim(left_parity, sec, 1)
    out_parity = lax.dynamic_slice_in_dim(right_parity, ops * 2, 2)
    live = ((out_parity + row_parity) % 2 == 1)[:, None, None]
    sends = left_products(lists, psi[:, 0], left_ops[0])
    blocks = [lax.all_to_all(send, "sec", 0, 0, tiled=True) for send in sends]
    (partial,) = right_products(lists, blocks[0], right_ops[0], True)
    early = lax.psum_scatter(partial, "ops", scatter_dimension=0, tiled=True)
    keep, give = right_products(lists, blocks[1], right_ops[0], False)
    late = summed_over_ops(keep, give).astype(BF16)
    result = jnp.concatenate([early, late], axis=1)
    return jnp.where(live, result, jnp.zeros_like(result))[None]


def solution(mesh):
    placed = (
        P(None, "sec", None, None),
        P("ops", None, None, None),
        P("ops", None),
        P("ops", None, None, None),
        P("ops", None),
        P(),
        P(),
    )
    return jax.shard_map(
        local, mesh=mesh, in_specs=placed, out_specs=P("sec", "ops", None, None), check_vma=False
    )
```

```python
import functools

import jax
import jax.numpy as jnp
from jax import lax
from jax.experimental import pallas as pl
from jax.experimental.pallas import tpu as pltpu
from jax.sharding import PartitionSpec as P

CHUNKS = (400, 112)
F32 = jnp.float32
BF16 = jnp.bfloat16
MIB = 1024 * 1024
AHEAD = 4
HBM = pl.BlockSpec(memory_space=pl.ANY)


def read_lists(given, held, sem):
    copies = [pltpu.make_async_copy(g, h, sem.at[n]) for n, (g, h) in enumerate(zip(given, held))]
    for copy in copies:
        copy.start()
    for copy in copies:
        copy.wait()


def list_scratch(k):
    return [pltpu.SMEM((k,), jnp.int32)] * 4 + [pltpu.SemaphoreType.DMA((4,))]


def note(need, item, source, carry, items, slots, fresh, seen):
    count, used = carry
    known = seen[source]
    new = (need & (known == 0)).astype(jnp.int32)

    @pl.when(need)
    def _():
        slot = jnp.where(known == 0, used, known - 1)
        items[count] = item
        slots[count] = slot
        fresh[count] = new
        seen[source] = slot + 1

    return count + need.astype(jnp.int32), used + new


def forget(seen, sectors):
    def clear(r, carry):
        seen[r] = 0
        return carry

    lax.fori_loop(0, sectors, clear, 0)


def left_kernel(*refs):
    lists, (psi, left), outs = refs[:4], refs[4:6], refs[6 : 6 + len(CHUNKS)]
    held, list_sem, items, slots, fresh, seen, pbuf, lbuf, obuf, psem, lsem, osem = refs[6 + len(CHUNKS):][:4], *refs[10 + len(CHUNKS):]
    read_lists(lists, held, list_sem)
    ls, rs, lp, rp = held
    sectors = psi.shape[0]
    col = lax.axis_index("sec")
    col_parity = rp[col] & 1

    def scan(k, flags):
        hit = (rs[k] == col).astype(jnp.int32)
        odd = rp[k] & 1
        return flags[0] | (hit * odd), flags[1] | (hit * (1 - odd))

    for_even, for_odd = lax.fori_loop(0, sectors, scan, (jnp.int32(0), jnp.int32(0)))

    forget(seen, sectors)

    def pick(i, carry):
        wanted = jnp.where((lp[i] & 1) == 1, for_odd, for_even)
        need = (wanted == 1) & ((lp[ls[i]] & 1) != col_parity)
        return note(need, i, ls[i], carry, items, slots, fresh, seen)

    count, _ = lax.fori_loop(0, sectors, pick, (jnp.int32(0), jnp.int32(0)))

    def fetch(j, carry=0):
        i = items[j]

        @pl.when(fresh[j] == 1)
        def _():
            pltpu.make_async_copy(psi.at[ls[i]], pbuf.at[slots[j]], psem.at[slots[j]]).start()

        pltpu.make_async_copy(left.at[i], lbuf.at[j], lsem.at[j]).start()
        return carry

    lax.fori_loop(0, jnp.minimum(count, AHEAD), fetch, 0)

    def stores(j):
        at = 0
        for c, rows in enumerate(CHUNKS):
            yield pltpu.make_async_copy(
                obuf.at[j, pl.ds(at, rows)], outs[c].at[items[j]], osem.at[c, j]
            )
            at += rows

    def work(j, carry):
        @pl.when(j + AHEAD < count)
        def _():
            fetch(j + AHEAD)

        @pl.when(fresh[j] == 1)
        def _():
            pltpu.make_async_copy(psi.at[0], pbuf.at[slots[j]], psem.at[slots[j]]).wait()

        pltpu.make_async_copy(left.at[0], lbuf.at[j], lsem.at[j]).wait()
        obuf[j] = jnp.dot(lbuf[j], pbuf[slots[j]], preferred_element_type=F32).astype(BF16)
        for copy in stores(j):
            copy.start()
        return carry

    lax.fori_loop(0, count, work, 0)

    def finish(j, carry):
        for copy in stores(j):
            copy.wait()
        return carry

    lax.fori_loop(0, count, finish, 0)


def left_products(lists, psi, left):
    k, m = psi.shape[0], psi.shape[-1]
    return pl.pallas_call(
        left_kernel,
        out_shape=[jax.ShapeDtypeStruct((k, rows, m), BF16) for rows in CHUNKS],
        in_specs=[HBM] * 6,
        out_specs=[HBM] * len(CHUNKS),
        scratch_shapes=list_scratch(k) + [
            pltpu.SMEM((k,), jnp.int32),
            pltpu.SMEM((k,), jnp.int32),
            pltpu.SMEM((k,), jnp.int32),
            pltpu.SMEM((k,), jnp.int32),
            pltpu.VMEM((k, m, m), BF16),
            pltpu.VMEM((k, m, m), BF16),
            pltpu.VMEM((k, m, m), BF16),
            pltpu.SemaphoreType.DMA((k,)),
            pltpu.SemaphoreType.DMA((k,)),
            pltpu.SemaphoreType.DMA((len(CHUNKS), k)),
        ],
        compiler_params=pltpu.CompilerParams(vmem_limit_bytes=56 * MIB),
        cost_estimate=pl.CostEstimate(
            flops=8 * m ** 3, bytes_accessed=12 * m * m * 2, transcendentals=0
        ),
        name="left_products",
    )(*lists, psi, left)


def right_kernel(whole, *refs):
    n = 7 if whole else 8
    lists, (block, right), outs, refs = refs[:4], refs[4:6], refs[6:n], refs[n:]
    held, (list_sem, items, slots, fresh, seen, zbuf, sbuf, rbuf, obuf, ssem, rsem, osem) = refs[:4], refs[4:]
    read_lists(lists, held, list_sem)
    ls, rs, lp, rp = held
    sectors = right.shape[0]
    row, core = lax.axis_index("sec"), lax.axis_index("ops") % 2
    row_parity = lp[row] & 1
    source_parity = lp[ls[row]] & 1
    zbuf[...] = jnp.zeros_like(zbuf)

    def place(buf, k):
        if whole:
            pltpu.make_async_copy(buf, outs[0].at[k], osem.at[k]).start()
            return
        keep, give = outs
        slot = (k // 4) * 2 + k % 2
        mine = (k // 2) % 2 == core

        @pl.when(mine)
        def _():
            pltpu.make_async_copy(buf, keep.at[slot], osem.at[k]).start()

        @pl.when(jnp.logical_not(mine))
        def _():
            pltpu.make_async_copy(buf, give.at[slot], osem.at[k]).start()

    forget(seen, sectors)

    def pick(k, carry):
        live = (rp[k] & 1) != row_parity
        need = live & ((rp[rs[k]] & 1) != source_parity)

        @pl.when(live & jnp.logical_not(need))
        def _():
            place(zbuf, k)

        return note(need, k, rs[k], carry, items, slots, fresh, seen)

    count, _ = lax.fori_loop(0, sectors, pick, (jnp.int32(0), jnp.int32(0)))

    def fetch(j, carry=0):
        k = items[j]
        pltpu.make_async_copy(right.at[k], rbuf.at[j], rsem.at[j]).start()

        @pl.when(fresh[j] == 1)
        def _():
            pltpu.make_async_copy(block.at[rs[k]], sbuf.at[slots[j]], ssem.at[slots[j]]).start()

        return carry

    lax.fori_loop(0, jnp.minimum(count, AHEAD), fetch, 0)

    def work(j, carry):
        @pl.when(j + AHEAD < count)
        def _():
            fetch(j + AHEAD)

        pltpu.make_async_copy(right.at[0], rbuf.at[j], rsem.at[j]).wait()

        @pl.when(fresh[j] == 1)
        def _():
            pltpu.make_async_copy(block.at[0], sbuf.at[slots[j]], ssem.at[slots[j]]).wait()

        obuf[j] = lax.dot_general(
            sbuf[slots[j]], rbuf[j], (((1,), (1,)), ((), ())), preferred_element_type=F32
        ).astype(BF16)
        place(obuf.at[j], items[j])
        return carry

    lax.fori_loop(0, count, work, 0)

    def finish(k, carry):
        @pl.when((rp[k] & 1) != row_parity)
        def _():
            pltpu.make_async_copy(zbuf, outs[0].at[0], osem.at[k]).wait()

        return carry

    lax.fori_loop(0, sectors, finish, 0)


def right_products(lists, block, right, whole):
    k, rows, m = block.shape
    out = [jax.ShapeDtypeStruct((k // 2, rows, m), BF16)] * 2
    if whole:
        out = [jax.ShapeDtypeStruct((k, rows, m), BF16)]
    return pl.pallas_call(
        functools.partial(right_kernel, whole),
        out_shape=out,
        in_specs=[HBM] * 6,
        out_specs=[HBM] * len(out),
        scratch_shapes=list_scratch(k) + [
            pltpu.SMEM((k,), jnp.int32),
            pltpu.SMEM((k,), jnp.int32),
            pltpu.SMEM((k,), jnp.int32),
            pltpu.SMEM((k,), jnp.int32),
            pltpu.VMEM((rows, m), BF16),
            pltpu.VMEM((k, rows, m), BF16),
            pltpu.VMEM((k, m, m), BF16),
            pltpu.VMEM((k, rows, m), BF16),
            pltpu.SemaphoreType.DMA((k,)),
            pltpu.SemaphoreType.DMA((k,)),
            pltpu.SemaphoreType.DMA((k,)),
        ],
        compiler_params=pltpu.CompilerParams(vmem_limit_bytes=61 * MIB),
        cost_estimate=pl.CostEstimate(
            flops=16 * rows * m * m, bytes_accessed=8 * m * m * 2 + 16 * rows * m * 2, transcendentals=0
        ),
        name="right_products",
    )(*lists, block, right)


def summed_over_ops(keep, give):
    n = 8
    got = lax.ppermute(give, "ops", [(o, o ^ 1) for o in range(n)])
    pair = (keep.astype(F32) + got.astype(F32)).astype(BF16)
    chip = lax.axis_index("ops") // 2
    total = lax.dynamic_slice_in_dim(pair, chip * 2, 2).astype(F32)
    for hop in (2, 1, 3):
        part = lax.dynamic_slice_in_dim(pair, (chip + hop) % 4 * 2, 2)
        part = lax.ppermute(part, "ops", [(o, (o + 2 * hop) % n) for o in range(n)])
        total = total + part.astype(F32)
    return total


def local(psi, left_ops, left_src, right_ops, right_src, left_parity, right_parity):
    sec, ops = lax.axis_index("sec"), lax.axis_index("ops")
    lists = (left_src[0], right_src[0], left_parity, right_parity)
    row_parity = lax.dynamic_slice_in_dim(left_parity, sec, 1)
    out_parity = lax.dynamic_slice_in_dim(right_parity, ops * 2, 2)
    live = ((out_parity + row_parity) % 2 == 1)[:, None, None]
    sends = left_products(lists, psi[:, 0], left_ops[0])
    blocks = [lax.all_to_all(send, "sec", 0, 0, tiled=True) for send in sends]
    (partial,) = right_products(lists, blocks[0], right_ops[0], True)
    early = lax.psum_scatter(partial, "ops", scatter_dimension=0, tiled=True)
    keep, give = right_products(lists, blocks[1], right_ops[0], False)
    late = jnp.where(live, summed_over_ops(keep, give), 0.0).astype(BF16)
    early = jnp.where(live, early, jnp.zeros_like(early))
    early = lax.optimization_barrier(jnp.pad(early, ((0, 0), (0, CHUNKS[1]), (0, 0))))
    return lax.dynamic_update_slice(early, late, (0, CHUNKS[0], 0))[None]


def solution(mesh):
    placed = (
        P(None, "sec", None, None),
        P("ops", None, None, None),
        P("ops", None),
        P("ops", None, None, None),
        P("ops", None),
        P(),
        P(),
    )
    return jax.shard_map(
        local, mesh=mesh, in_specs=placed, out_specs=P("sec", "ops", None, None), check_vma=False
    )
```

```python
import functools

import jax
import jax.numpy as jnp
from jax import lax
from jax.experimental import pallas as pl
from jax.experimental.pallas import tpu as pltpu
from jax.sharding import PartitionSpec as P

CHUNKS = (400, 112)
F32 = jnp.float32
BF16 = jnp.bfloat16
MIB = 1024 * 1024
AHEAD = 4
HBM = pl.BlockSpec(memory_space=pl.ANY)


def read_lists(given, held, sem):
    copies = [pltpu.make_async_copy(g, h, sem.at[n]) for n, (g, h) in enumerate(zip(given, held))]
    for copy in copies:
        copy.start()
    for copy in copies:
        copy.wait()


def list_scratch(k):
    return [pltpu.SMEM((k,), jnp.int32)] * 4 + [pltpu.SemaphoreType.DMA((4,))]


def note(need, item, source, carry, items, slots, fresh, seen):
    count, used = carry
    known = seen[source]
    new = (need & (known == 0)).astype(jnp.int32)

    @pl.when(need)
    def _():
        slot = jnp.where(known == 0, used, known - 1)
        items[count] = item
        slots[count] = slot
        fresh[count] = new
        seen[source] = slot + 1

    return count + need.astype(jnp.int32), used + new


def forget(seen, sectors):
    def clear(r, carry):
        seen[r] = 0
        return carry

    lax.fori_loop(0, sectors, clear, 0, unroll=True)


def left_kernel(*refs):
    lists, (psi, left), outs = refs[:4], refs[4:6], refs[6 : 6 + len(CHUNKS)]
    held, list_sem, items, slots, fresh, seen, pbuf, lbuf, obuf, psem, lsem, osem = refs[6 + len(CHUNKS):][:4], *refs[10 + len(CHUNKS):]
    read_lists(lists, held, list_sem)
    ls, rs, lp, rp = held
    sectors = psi.shape[0]
    col = lax.axis_index("sec")
    col_parity = rp[col] & 1

    def scan(k, flags):
        hit = (rs[k] == col).astype(jnp.int32)
        odd = rp[k] & 1
        return flags[0] | (hit * odd), flags[1] | (hit * (1 - odd))

    for_even, for_odd = lax.fori_loop(0, sectors, scan, (jnp.int32(0), jnp.int32(0)), unroll=True)

    forget(seen, sectors)

    def pick(i, carry):
        wanted = jnp.where((lp[i] & 1) == 1, for_odd, for_even)
        need = (wanted == 1) & ((lp[ls[i]] & 1) != col_parity)
        return note(need, i, ls[i], carry, items, slots, fresh, seen)

    count, _ = lax.fori_loop(0, sectors, pick, (jnp.int32(0), jnp.int32(0)), unroll=True)

    def fetch(j, carry=0):
        i = items[j]

        @pl.when(fresh[j] == 1)
        def _():
            pltpu.make_async_copy(psi.at[ls[i]], pbuf.at[slots[j]], psem.at[slots[j]]).start()

        pltpu.make_async_copy(left.at[i], lbuf.at[j], lsem.at[j]).start()
        return carry

    lax.fori_loop(0, jnp.minimum(count, AHEAD), fetch, 0)

    def stores(j):
        at = 0
        for c, rows in enumerate(CHUNKS):
            yield pltpu.make_async_copy(
                obuf.at[j, pl.ds(at, rows)], outs[c].at[items[j]], osem.at[c, j]
            )
            at += rows

    def work(j, carry):
        @pl.when(j + AHEAD < count)
        def _():
            fetch(j + AHEAD)

        @pl.when(fresh[j] == 1)
        def _():
            pltpu.make_async_copy(psi.at[0], pbuf.at[slots[j]], psem.at[slots[j]]).wait()

        pltpu.make_async_copy(left.at[0], lbuf.at[j], lsem.at[j]).wait()
        obuf[j] = jnp.dot(lbuf[j], pbuf[slots[j]], preferred_element_type=F32).astype(BF16)
        for copy in stores(j):
            copy.start()
        return carry

    lax.fori_loop(0, count, work, 0)

    def finish(j, carry):
        for copy in stores(j):
            copy.wait()
        return carry

    lax.fori_loop(0, count, finish, 0)


def left_products(lists, psi, left):
    k, m = psi.shape[0], psi.shape[-1]
    return pl.pallas_call(
        left_kernel,
        out_shape=[jax.ShapeDtypeStruct((k, rows, m), BF16) for rows in CHUNKS],
        in_specs=[HBM] * 6,
        out_specs=[HBM] * len(CHUNKS),
        scratch_shapes=list_scratch(k) + [
            pltpu.SMEM((k,), jnp.int32),
            pltpu.SMEM((k,), jnp.int32),
            pltpu.SMEM((k,), jnp.int32),
            pltpu.SMEM((k,), jnp.int32),
            pltpu.VMEM((k, m, m), BF16),
            pltpu.VMEM((k, m, m), BF16),
            pltpu.VMEM((k, m, m), BF16),
            pltpu.SemaphoreType.DMA((k,)),
            pltpu.SemaphoreType.DMA((k,)),
            pltpu.SemaphoreType.DMA((len(CHUNKS), k)),
        ],
        compiler_params=pltpu.CompilerParams(vmem_limit_bytes=56 * MIB),
        cost_estimate=pl.CostEstimate(
            flops=8 * m ** 3, bytes_accessed=12 * m * m * 2, transcendentals=0
        ),
        name="left_products",
    )(*lists, psi, left)


def right_kernel(whole, *refs):
    n = 7 if whole else 8
    lists, (block, right), outs, refs = refs[:4], refs[4:6], refs[6:n], refs[n:]
    held, (list_sem, items, slots, fresh, seen, zbuf, sbuf, rbuf, obuf, ssem, rsem, osem) = refs[:4], refs[4:]
    read_lists(lists, held, list_sem)
    ls, rs, lp, rp = held
    sectors = right.shape[0]
    row, core = lax.axis_index("sec"), lax.axis_index("ops") % 2
    row_parity = lp[row] & 1
    source_parity = lp[ls[row]] & 1
    zbuf[...] = jnp.zeros_like(zbuf)

    def place(buf, k):
        if whole:
            pltpu.make_async_copy(buf, outs[0].at[k], osem.at[k]).start()
            return
        keep, give = outs
        slot = (k // 4) * 2 + k % 2
        mine = (k // 2) % 2 == core

        @pl.when(mine)
        def _():
            pltpu.make_async_copy(buf, keep.at[slot], osem.at[k]).start()

        @pl.when(jnp.logical_not(mine))
        def _():
            pltpu.make_async_copy(buf, give.at[slot], osem.at[k]).start()

    forget(seen, sectors)

    def pick(k, carry):
        live = (rp[k] & 1) != row_parity
        need = live & ((rp[rs[k]] & 1) != source_parity)

        @pl.when(live & jnp.logical_not(need))
        def _():
            place(zbuf, k)

        return note(need, k, rs[k], carry, items, slots, fresh, seen)

    count, _ = lax.fori_loop(0, sectors, pick, (jnp.int32(0), jnp.int32(0)), unroll=True)

    def fetch(j, carry=0):
        k = items[j]
        pltpu.make_async_copy(right.at[k], rbuf.at[j], rsem.at[j]).start()

        @pl.when(fresh[j] == 1)
        def _():
            pltpu.make_async_copy(block.at[rs[k]], sbuf.at[slots[j]], ssem.at[slots[j]]).start()

        return carry

    lax.fori_loop(0, jnp.minimum(count, AHEAD), fetch, 0)

    def work(j, carry):
        @pl.when(j + AHEAD < count)
        def _():
            fetch(j + AHEAD)

        pltpu.make_async_copy(right.at[0], rbuf.at[j], rsem.at[j]).wait()

        @pl.when(fresh[j] == 1)
        def _():
            pltpu.make_async_copy(block.at[0], sbuf.at[slots[j]], ssem.at[slots[j]]).wait()

        obuf[j] = lax.dot_general(
            sbuf[slots[j]], rbuf[j], (((1,), (1,)), ((), ())), preferred_element_type=F32
        ).astype(BF16)
        place(obuf.at[j], items[j])
        return carry

    lax.fori_loop(0, count, work, 0)

    def finish(k, carry):
        @pl.when((rp[k] & 1) != row_parity)
        def _():
            pltpu.make_async_copy(zbuf, outs[0].at[0], osem.at[k]).wait()

        return carry

    lax.fori_loop(0, sectors, finish, 0, unroll=True)


def right_products(lists, block, right, whole):
    k, rows, m = block.shape
    out = [jax.ShapeDtypeStruct((k // 2, rows, m), BF16)] * 2
    if whole:
        out = [jax.ShapeDtypeStruct((k, rows, m), BF16)]
    return pl.pallas_call(
        functools.partial(right_kernel, whole),
        out_shape=out,
        in_specs=[HBM] * 6,
        out_specs=[HBM] * len(out),
        scratch_shapes=list_scratch(k) + [
            pltpu.SMEM((k,), jnp.int32),
            pltpu.SMEM((k,), jnp.int32),
            pltpu.SMEM((k,), jnp.int32),
            pltpu.SMEM((k,), jnp.int32),
            pltpu.VMEM((rows, m), BF16),
            pltpu.VMEM((k, rows, m), BF16),
            pltpu.VMEM((k, m, m), BF16),
            pltpu.VMEM((k, rows, m), BF16),
            pltpu.SemaphoreType.DMA((k,)),
            pltpu.SemaphoreType.DMA((k,)),
            pltpu.SemaphoreType.DMA((k,)),
        ],
        compiler_params=pltpu.CompilerParams(vmem_limit_bytes=61 * MIB),
        cost_estimate=pl.CostEstimate(
            flops=16 * rows * m * m, bytes_accessed=8 * m * m * 2 + 16 * rows * m * 2, transcendentals=0
        ),
        name="right_products",
    )(*lists, block, right)


def summed_over_ops(keep, give):
    n = 8
    got = lax.ppermute(give, "ops", [(o, o ^ 1) for o in range(n)])
    pair = (keep.astype(F32) + got.astype(F32)).astype(BF16)
    chip = lax.axis_index("ops") // 2
    total = lax.dynamic_slice_in_dim(pair, chip * 2, 2).astype(F32)
    for hop in (2, 1, 3):
        part = lax.dynamic_slice_in_dim(pair, (chip + hop) % 4 * 2, 2)
        part = lax.ppermute(part, "ops", [(o, (o + 2 * hop) % n) for o in range(n)])
        total = total + part.astype(F32)
    return total


def local(psi, left_ops, left_src, right_ops, right_src, left_parity, right_parity):
    sec, ops = lax.axis_index("sec"), lax.axis_index("ops")
    lists = (left_src[0], right_src[0], left_parity, right_parity)
    row_parity = lax.dynamic_slice_in_dim(left_parity, sec, 1)
    out_parity = lax.dynamic_slice_in_dim(right_parity, ops * 2, 2)
    live = ((out_parity + row_parity) % 2 == 1)[:, None, None]
    sends = left_products(lists, psi[:, 0], left_ops[0])
    blocks = [lax.all_to_all(send, "sec", 0, 0, tiled=True) for send in sends]
    (partial,) = right_products(lists, blocks[0], right_ops[0], True)
    early = lax.psum_scatter(partial, "ops", scatter_dimension=0, tiled=True)
    keep, give = right_products(lists, blocks[1], right_ops[0], False)
    late = jnp.where(live, summed_over_ops(keep, give), 0.0).astype(BF16)
    early = jnp.where(live, early, jnp.zeros_like(early))
    early = lax.optimization_barrier(jnp.pad(early, ((0, 0), (0, CHUNKS[1]), (0, 0))))
    return lax.dynamic_update_slice(early, late, (0, CHUNKS[0], 0))[None]


def solution(mesh):
    placed = (
        P(None, "sec", None, None),
        P("ops", None, None, None),
        P("ops", None),
        P("ops", None, None, None),
        P("ops", None),
        P(),
        P(),
    )
    return jax.shard_map(
        local, mesh=mesh, in_specs=placed, out_specs=P("sec", "ops", None, None), check_vma=False
    )
```
